32 devices in a mesh: rep: 16 (over z, y, core), shard: 2 (over x).
Axes of the slice: x: 2, y: 2, z: 4, core: 2. Of those that a mesh axis runs over, the one named last changes fastest.
Arguments:
- hidden_in: bfloat16 [32768, 1536], P(('rep', 'shard')), may hold values from -6 to 6
- segment_ids: int32 [32, 1024], P(('rep', 'shard')), may hold values from 0 to 3, never falling along the last dimension, each value on 1 to 512 neighbouring positions
- norm_gain: float32 [1536], P('shard'), may hold values from 0.25 to 1.75
- in_weight: bfloat16 [1536, 6448], P('shard'), may hold values from -0.15625 to 0.15625
- conv_weight: float32 [4, 3328], P(None, 'shard'), may hold values from -3 to 3
- conv_bias: float32 [3328], P('shard'), may hold values from -3 to 3
- dt_bias: float32 [48], P('shard'), may hold values from -5 to -1.5
- a_log: float32 [48], P('shard'), may hold values from 0 to 2.77
- d_skip: float32 [48], P('shard'), may hold values from 0.3 to 1.7
- gate_gain: float32 [3072], P('shard'), may hold values from 0.25 to 1.75
- out_weight: bfloat16 [3072, 1536], P('shard'), may hold values from -0.109375 to 0.109375
- cotangent: bfloat16 [32768, 1536], P(('rep', 'shard')), may hold values from -6 to 6
Outputs:
- block_out: bfloat16 [32768, 1536], P(('rep', 'shard'))
- input_grad: float32 [32768, 1536], P(('rep', 'shard'))
- grad_norm_gain: float32 [1536], P('shard')
- grad_in_weight: float32 [1536, 6448], P('shard')
- grad_conv_weight: float32 [4, 3328], P(None, 'shard')
- grad_conv_bias: float32 [3328], P('shard')
- grad_dt_bias: float32 [48], P('shard')
- grad_a_log: float32 [48], P('shard')
- grad_d_skip: float32 [48], P('shard')
- grad_gate_gain: float32 [3072], P('shard')
- grad_out_weight: float32 [3072, 1536], P('shard')
The draws below stay inside these ranges and needn't reach their ends.
Inputs may be any that keep to these rules, and one draw needn't show every extreme that they name: `segment_ids`: in each packed row the numbers never fall, each of 0 to 3 occurs in one run of 1 to 512 tokens, and one run has exactly 512.
All inputs are finite; a program needn't handle non-finite values.
Results may differ from the reference program's by a relative error of at most 0.0075.
Values may be sent and summed in bfloat16 or wider, within the bound.
A program may use at most 384 MiB of HBM per device.

```python
import math
import jax
import jax.numpy as jnp
import numpy as np
from jax import lax

D = 1536
H = 48
HEADDIM = 64
N = 128
CONV = 4
SPAN = 256
ROW_LEN = 1024
SEGS = 4
DI = 3072
CW = 3328
P_SIZE = 6448
MOST_SEG = 512
ROWS = 32
TOKENS = 32768


def block_scale(rng, extent, shards, low, largest):
    loudness, own = 1.0, jax.random.fold_in(rng, 6)
    for axis_at, parts in shards:
        steps = jnp.exp(jax.random.uniform(jax.random.fold_in(own, axis_at), (parts,), jnp.float32, low / len(shards), largest / len(shards)))
        loudness = loudness * jnp.repeat(steps, extent[axis_at] // parts).reshape([-1 if axis == axis_at else 1 for axis in range(len(extent))])
    return loudness


def length_profile(count, total, bound, lean):
    loads = [(1 << 20) // math.isqrt(standing ** lean) + 1 for standing in range(2, count + 1)]
    surplus, holding = total - bound - (count - 1), [1] * (count - 1)
    while surplus > 0:
        movable = [i for i in range(count - 1) if holding[i] < bound]
        pool, remaining = sum([loads[i] for i in movable]), surplus
        for i in movable:
            extra = min(bound - holding[i], max(1, remaining * loads[i] // pool), surplus)
            holding[i] = holding[i] + extra
            surplus = surplus - extra
    return np.array([bound] + holding)


def ragged_sizes(stream_key, count, total, limit, lean):
    if count == 2:
        one = jax.random.randint(stream_key, (), max(1, total - limit), min(limit, total - 1) + 1)
        return jnp.stack([one, total - one])
    sizes = jnp.asarray(length_profile(count, total, limit, lean), jnp.int32)
    twos = (count - 1) // 2
    giver, receiver = sizes[1:1 + 2 * twos:2], sizes[2:2 + 2 * twos:2]
    margin = jnp.minimum(giver - 1, limit - receiver)
    passed = jax.random.randint(jax.random.fold_in(stream_key, 1), (twos,), 0, 1 << 20) % (margin + 1)
    sizes = sizes.at[1:1 + 2 * twos:2].set(giver - passed).at[2:2 + 2 * twos:2].set(receiver + passed)
    return sizes[jax.random.permutation(jax.random.fold_in(stream_key, 2), count)]


def scatter_about(key, dims, deviation, limit, shards=(), held_as=jnp.bfloat16):
    gain = block_scale(key, dims, shards, -0.22, 0.18) if shards else 1.0
    entries = jax.random.normal(key, dims, jnp.float32) * deviation * gain
    return jnp.minimum(jnp.maximum(entries, -limit), limit).astype(held_as)


def setup_inputs(seed: int = 0) -> dict:
    seeds = jax.random.split(jax.random.key(seed), 13)
    hidden_in = scatter_about(seeds[0], (TOKENS, D), 1.0, 6.0, ((0, 32),))
    segment_ids = jax.vmap(lambda own: jnp.searchsorted(jnp.cumsum(ragged_sizes(own, SEGS, ROW_LEN, MOST_SEG, 0)), jnp.arange(ROW_LEN), side="right"))(jax.random.split(seeds[1], ROWS)).reshape((ROWS, ROW_LEN)).astype(jnp.int32)
    norm_gain = jnp.clip(1.0 + 0.15 * jax.random.normal(seeds[2], (D,), jnp.float32), 0.25, 1.75)
    in_weight = scatter_about(seeds[3], (D, P_SIZE), D ** -0.5, 0.15625, ((0, 2),))
    conv_weight = scatter_about(seeds[4], (CONV, CW), CONV ** -0.5, 3.0, ((1, 2),), jnp.float32)
    conv_bias = scatter_about(seeds[5], (CW,), 0.5, 3.0, ((0, 2),), jnp.float32)
    dt_bias = jnp.clip(-5.0 + 3.5 * jax.random.uniform(seeds[6], (H,), jnp.float32) ** block_scale(seeds[6], (H,), ((0, 2),), -0.2, 0.2), -5.0, -1.5)
    a_log = jnp.clip(2.77 * jax.random.uniform(seeds[7], (H,), jnp.float32) ** block_scale(seeds[7], (H,), ((0, 2),), -0.2, 0.2), 0.0, 2.77)
    d_skip = jnp.clip(0.3 + 1.40000004 * jax.random.uniform(seeds[8], (H,), jnp.float32) ** block_scale(seeds[8], (H,), ((0, 2),), -0.2, 0.2), 0.3, 1.7)
    gate_gain = jnp.clip(1.0 + 0.15 * jax.random.normal(seeds[9], (DI,), jnp.float32), 0.25, 1.75)
    out_weight = scatter_about(seeds[10], (DI, D), DI ** -0.5, 0.109375, ((0, 2),))
    cotangent = scatter_about(seeds[11], (TOKENS, D), 1.0, 6.0, ((0, 32),))
    return dict(hidden_in=hidden_in, segment_ids=segment_ids, norm_gain=norm_gain, in_weight=in_weight, conv_weight=conv_weight, conv_bias=conv_bias, dt_bias=dt_bias, a_log=a_log, d_skip=d_skip, gate_gain=gate_gain, out_weight=out_weight, cotangent=cotangent)


@jax.custom_vjp
def low(v):
    return lax.optimization_barrier(v.astype(jnp.bfloat16)).astype(jnp.float32)

@jax.custom_vjp
def low_back(v):
    return v

def low_keep(v):
    return (low(v), None)

def low_pass(kept, grad):
    return (grad,)

def back_keep(v):
    return (v, None)

def back_low(kept, grad):
    return (low(grad),)
low.defvjp(low_keep, low_pass)
low_back.defvjp(back_keep, back_low)
EPS = 1e-05
HIGH = lax.Precision.HIGHEST

def conv_row(channels, segments, conv_weight, conv_bias):
    length = channels.shape[0]
    padded = jnp.concatenate([jnp.zeros((CONV - 1, channels.shape[1]), jnp.float32), channels], axis=0)
    seg_padded = jnp.concatenate([jnp.full((CONV - 1,), -1, jnp.int32), segments.astype(jnp.int32)], axis=0)
    summed = conv_bias[None, :] + jnp.zeros_like(channels)
    for offset in range(CONV):
        same_seg = (seg_padded[offset:offset + length] == segments).astype(jnp.float32)
        summed = summed + conv_weight[offset][None, :] * padded[offset:offset + length] * same_seg[:, None]
    return summed

def span_step(carry, block):
    state, seg_prev = carry
    signal, steps_dt, log_decay, inputs_b, readout, segments = block
    cumulated = jnp.cumsum(log_decay, axis=0)
    count = segments.shape[0]
    position = jnp.arange(count)
    causal = (position[:, None] >= position[None, :]) & (segments[:, None] == segments[None, :])
    spread_log = cumulated.T[:, :, None] - cumulated.T[:, None, :]
    decayed = jnp.exp(jnp.where(causal[None], spread_log, -1e+30))
    scores = jnp.dot(readout, inputs_b.T, precision=HIGH)
    scaled_x = signal * steps_dt[:, :, None]
    within = jnp.einsum('hts,shp->thp', decayed * scores[None], scaled_x, precision=HIGH)
    carried = (segments == seg_prev).astype(jnp.float32)
    from_state = jnp.einsum('tn,hpn->thp', readout, state, precision=HIGH) * (jnp.exp(cumulated) * carried[:, None])[:, :, None]
    last_seg = segments[count - 1]
    to_end = jnp.exp(cumulated[count - 1][None, :] - cumulated) * (segments == last_seg).astype(jnp.float32)[:, None]
    kept_share = jnp.exp(cumulated[count - 1]) * (last_seg == seg_prev).astype(jnp.float32)
    new_state = state * kept_share[:, None, None] + jnp.einsum('sh,shp,sn->hpn', to_end, scaled_x, inputs_b, precision=HIGH)
    return ((new_state, last_seg), within + from_state)

def scan_row(signal, steps_dt, log_decay, inputs_b, readout, segments):
    blocks = signal.shape[0] // SPAN

    def split(value):
        return value.reshape((blocks, SPAN) + value.shape[1:])
    start_state = jnp.zeros((H, HEADDIM, N), jnp.float32)
    _, outputs = lax.scan(jax.checkpoint(span_step), (start_state, segments[0]), (split(signal), split(steps_dt), split(log_decay), split(inputs_b), split(readout), split(segments)))
    return outputs.reshape(signal.shape)

def mixer_row(gate_z, channels, dt_raw, segments, conv_weight, conv_bias, dt_bias, a_log, d_skip, gate_gain):
    length = gate_z.shape[0]
    inner = H * HEADDIM
    activated = jax.nn.silu(conv_row(channels, segments, conv_weight, conv_bias))
    signal = activated[:, :inner].reshape(length, H, HEADDIM)
    inputs_b = activated[:, inner:inner + N]
    readout = activated[:, inner + N:]
    steps_dt = jax.nn.softplus(dt_raw + dt_bias[None, :])
    log_decay = -jnp.exp(a_log)[None, :] * steps_dt
    outputs = scan_row(signal, steps_dt, log_decay, inputs_b, readout, segments) + d_skip[None, :, None] * signal
    gated = outputs.reshape(length, inner) * jax.nn.silu(gate_z)
    factor = lax.rsqrt(lax.optimization_barrier(jnp.mean(gated * gated, axis=1, keepdims=True)) + EPS)
    return gated * factor * gate_gain[None, :]

def mixer_rows(mixed, segment_ids, conv_weight, conv_bias, dt_bias, a_log, d_skip, gate_gain):
    rows, length = segment_ids.shape
    inner = H * HEADDIM
    width = conv_weight.shape[1]
    grouped = mixed.reshape(rows, length, mixed.shape[1])

    def one_row(block, segments):
        return mixer_row(block[:, :inner], block[:, inner:inner + width], block[:, inner + width:], segments, conv_weight, conv_bias, dt_bias, a_log, d_skip, gate_gain)
    return jax.vmap(one_row)(grouped, segment_ids).reshape(rows * length, inner)

def branch(hidden, segments, norm_gain, in_weight, conv_weight, conv_bias, dt_bias, a_log, d_skip, gate_gain, out_weight):
    factor = lax.rsqrt(lax.optimization_barrier(jnp.mean(hidden * hidden, axis=1, keepdims=True)) + EPS)
    normed = low(hidden * factor * norm_gain[None, :])
    mixed = low_back(jnp.dot(normed, in_weight, precision=HIGH))
    gnormed = mixer_rows(mixed, segments, conv_weight, conv_bias, dt_bias, a_log, d_skip, gate_gain)
    return low_back(jnp.dot(low(gnormed), out_weight, precision=HIGH))

def reference(hidden_in, segment_ids, norm_gain, in_weight, conv_weight, conv_bias, dt_bias, a_log, d_skip, gate_gain, out_weight, cotangent):
    group = 4 if ROWS % 4 == 0 else 1
    hidden = hidden_in.astype(jnp.float32)
    grouped_segs = segment_ids.reshape(ROWS // group, group, ROW_LEN)

    def whole(hidden, norm_gain, in_weight, conv_weight, conv_bias, dt_bias, a_log, d_skip, gate_gain, out_weight):
        grouped = hidden.reshape(ROWS // group, group * ROW_LEN, D)

        def one_group(item):
            return jax.checkpoint(branch)(item[0], item[1], norm_gain, in_weight, conv_weight, conv_bias, dt_bias, a_log, d_skip, gate_gain, out_weight)
        return hidden + lax.map(one_group, (grouped, grouped_segs)).reshape(TOKENS, D)
    result, pullback = jax.vjp(whole, hidden, norm_gain, in_weight.astype(jnp.float32), conv_weight, conv_bias, dt_bias, a_log, d_skip, gate_gain, out_weight.astype(jnp.float32))
    grads = pullback(cotangent.astype(jnp.float32))
    return (result.astype(jnp.bfloat16), grads[0], grads[1], grads[2], grads[3], grads[4], grads[5], grads[6], grads[7], grads[8], grads[9])
```

```python
import functools

import jax
import jax.numpy as jnp
import numpy as np
from jax import lax
from jax.experimental import pallas as pl
from jax.experimental.pallas import tpu as pltpu
from jax.sharding import PartitionSpec as P

D = 1536
H = 48
HEADDIM = 64
N = 128
CONV = 4
DI = 3072
CW = 3328
XD = 3456
Q = 128
GW = 256
EPS = 1e-05
F32 = jnp.float32
BF = jnp.bfloat16
HIGH = lax.Precision.HIGHEST


def dot(a, b):
    return jnp.dot(a, b, preferred_element_type=F32)


def dot_nt(a, b):
    return lax.dot_general(a, b, (((1,), (1,)), ((), ())), preferred_element_type=F32)


def iota(shape, dim):
    return lax.broadcasted_iota(jnp.int32, shape, dim)


def sigmoid(v):
    return 0.5 * jnp.tanh(0.5 * v) + 0.5


def softplus(v):
    return jnp.maximum(v, 0.0) + jnp.log1p(jnp.exp(-jnp.abs(v)))


def params(limit):
    return pltpu.CompilerParams(
        dimension_semantics=("arbitrary",), vmem_limit_bytes=limit << 20
    )


def spread_consts():
    head_of = np.arange(DI) // HEADDIM
    ind = np.zeros((128, DI), np.float32)
    ind[head_of, np.arange(DI)] = 1
    ind[64 + head_of, np.arange(DI)] = 1
    wide = np.arange(H * Q) // Q
    ind2 = np.zeros((256, H * Q), np.float32)
    for at in (0, 64, 128):
        ind2[at + wide, np.arange(H * Q)] = 1
    ind_t = np.zeros((DI, 128), np.float32)
    ind_t[np.arange(DI), head_of] = 1
    rho_t = np.zeros((H * Q, 128), np.float32)
    rho_t[np.arange(H * Q), wide] = 1
    return [jnp.asarray(v, BF) for v in (ind, ind2, ind_t, rho_t)]


def prep_kernel(raw_ref, prm_ref, segc_ref, cum3_ref, ex_ref, cumt_ref):
    head = iota((Q, 128), 1) < H
    tri = (iota((Q, Q), 0) >= iota((Q, Q), 1)).astype(F32)
    bias = prm_ref[6:7, :128]
    rate = -jnp.exp(prm_ref[7:8, :128])

    def high(v):
        return v.astype(BF).astype(F32)

    def two(v):
        top = high(v)
        return (top + pltpu.roll(high(v - top), 64, axis=1)).astype(BF)

    for c in range(raw_ref.shape[0] // Q):
        rows = slice(c * Q, (c + 1) * Q)
        dt = jnp.where(head, softplus(raw_ref[rows, :] + bias), 0.0)
        cum = jnp.dot(tri, dt * rate, precision=HIGH, preferred_element_type=F32)
        cum = jnp.where(head, cum, 0.0)
        top = high(cum)
        mid = high(cum - top)
        low = high(cum - top - mid)
        cum3_ref[rows, :128] = (top + pltpu.roll(mid, 64, axis=1)).astype(BF)
        cum3_ref[rows, 128:] = low.astype(BF)
        carried = jnp.exp(cum) * segc_ref[rows, 4:5]
        to_end = jnp.exp(cum[Q - 1 : Q, :] - cum) * segc_ref[rows, 5:6]
        ex_ref[c, 0:Q, :] = two(dt)
        ex_ref[c, Q : 2 * Q, :] = two(jnp.where(head, carried, 0.0))
        ex_ref[c, 2 * Q :, :] = two(jnp.where(head, to_end, 0.0))
        cumt_ref[c] = cum.T[:H, :]


def prep(raw, prm, segc):
    tokens = raw.shape[0]
    chunks = tokens // Q
    return pl.pallas_call(
        prep_kernel,
        grid=(1,),
        in_specs=[
            pl.BlockSpec((tokens, 128), lambda i: (0, 0)),
            pl.BlockSpec((8, XD), lambda i: (0, 0)),
            pl.BlockSpec((tokens, 16), lambda i: (0, 0)),
        ],
        out_specs=[
            pl.BlockSpec((tokens, 256), lambda i: (0, 0)),
            pl.BlockSpec((chunks, 3 * Q, 128), lambda i: (0, 0, 0)),
            pl.BlockSpec((chunks, H, Q), lambda i: (0, 0, 0)),
        ],
        out_shape=[
            jax.ShapeDtypeStruct((tokens, 256), BF),
            jax.ShapeDtypeStruct((chunks, 3 * Q, 128), BF),
            jax.ShapeDtypeStruct((chunks, H, Q), F32),
        ],
        compiler_params=params(60),
        name="prep",
    )(raw, prm, segc)


VEC = 88


class Place:
    def __init__(self):
        self.rep, self.shard = lax.axis_index("rep"), lax.axis_index("shard")
        self.bits = lax.axis_size("rep").bit_length() - 1

    def bit(self, k):
        return (self.rep // (1 << k)) % 2

    def partner(self, k):
        if k == "x":
            return {"shard": 1 - self.shard}
        return {"rep": self.rep + (1 - 2 * self.bit(k)) * (1 << k)}

    def greet(self, keys):
        barrier = pltpu.get_barrier_semaphore()
        for k in keys:
            pl.semaphore_signal(
                barrier, inc=1, device_id=self.partner(k), device_id_type=pl.DeviceIdType.MESH
            )
        pl.semaphore_wait(barrier, len(keys))


class SemPool:
    def __init__(self, ref):
        self.ref, self.used = ref, 0

    def reserve(self, count):
        self.used += count
        return self.used - count


def in_two(ref):
    if len(ref.shape) > 2:
        return [ref.at[0], ref.at[1]] if ref.shape[0] == 2 else [ref]
    rows = ref.shape[0] // 2
    return [ref.at[pl.ds(0, rows)], ref.at[pl.ds(rows, rows)]] if rows % 16 == 0 else [ref]


def copiers(me, sems, base, count):
    sem = iter(range(count))
    at = lambda: sems.at[base + next(sem)]

    def remote(src, dst, key):
        return [
            pltpu.make_async_remote_copy(
                a, b, at(), at(), device_id=me.partner(key), device_id_type=pl.DeviceIdType.MESH
            )
            for a, b in zip(in_two(src), in_two(dst))
        ]

    def local(src, dst):
        return [pltpu.make_async_copy(src, dst, at())]

    return remote, local


class Chain:
    def claim(self, me, sems, name):
        self.me, self.sems, self.name = me, sems, name
        self.base = [sems.reserve(12) for _ in self.phases]

    def build(self, step):
        return self.copies(step, *copiers(self.me, self.sems.ref, self.base[step], 12))

    def start(self, step):
        for copy in self.build(step):
            copy.start()

    def finish(self, step):
        for copy in self.build(step):
            copy.wait()
        self.then(step)

    def then(self, step):
        pass


RATE = 0.085
HOP = 2.5


class Rows(Chain):
    def __init__(self, me, sems, name, src, full, low, count, order):
        self.src, self.full, self.rows, self.order = src, full, pl.ds(low, count), order
        self.size = 2 * 2 * count * full.shape[-1] / 1e6
        self.phases = ["x", order[0], order[1], "core"]
        self.claim(me, sems, name)

    def copies(self, step, remote, local):
        me, full = self.me, self.full
        b1, b2, core = me.bit(1), me.bit(2), me.bit(0)
        every = slice(None)
        at = {
            0: (b1, b2, core),
            1: (b1, b2, core),
            2: (every, b2, core) if self.order[0] == 1 else (b1, every, core),
            3: (every, every, core),
        }[step]
        part = full.at[at + (self.rows, every)]
        if step == 0:
            return remote(self.src((b1 * 2 + b2) * 2 + core), part, "x")
        return remote(part, part, 0 if step == 3 else self.order[step - 1])

    def cost(self, step):
        link = self.phases[step]
        if link == "core":
            return [(link, 4 * self.size / 2 / 0.2)]
        return [(link, (1, 1, 2)[step] * self.size / RATE)]


class Item(Chain):
    def __init__(
        self, me, sems, name, part, order, back, splits, shape, refs, src=None, dst=None, hand=None
    ):
        self.splits, self.shape = splits, shape
        self.order = list(order) + list(range(len(order), me.bits))
        self.back = [k for k in back if k <= splits]
        self.src, self.dst, self.hand = src, dst, hand
        self.keys = ["x"] + list(range(1, splits + 1))
        self.phases = []
        if part != "late":
            self.phases += self.order
        self.phases += {"early": ["store"], "late": ["load"], "all": []}[part]
        if part != "early":
            self.phases += [("back", k) for k in self.back] + ["out"]
        if refs is not None:
            self.bufs = self.take(refs, part)
        self.claim(me, sems, name)

    @staticmethod
    def shapes(bits, part, order, splits, shape):
        own = (2,) * splits
        out = [pltpu.VMEM(own + shape, BF)]
        if part == "late":
            return out
        out.append(pltpu.VMEM(own + shape, BF))
        free = splits + 1
        for k in list(order) + list(range(len(order), bits)):
            free -= k == "x" or k <= splits
            out.append(pltpu.VMEM((2,) * free + shape, BF))
        return out

    def take(self, refs, part):
        bufs = dict(all=refs.pop(0))
        if part != "late":
            bufs["acc"] = refs.pop(0)
            for k in self.order:
                bufs[k] = refs.pop(0)
        return bufs

    def own(self, key):
        return self.me.shard if key == "x" else self.me.bit(key)

    def place(self, done, key=None):
        out = []
        for k in self.keys:
            if k == self.order[0]:
                continue
            if k in done:
                out.append(self.own(k))
            else:
                out.append(1 - self.own(k) if k == key else slice(None))
        return tuple(out)

    def gathered(self, back):
        return tuple(
            slice(None) if k in back else self.own(k) for k in range(1, self.splits + 1)
        )

    def copies(self, step, remote, local):
        me, phase, bufs = self.me, self.phases[step], self.bufs
        if phase == "store":
            return local(bufs["all"].at[self.gathered(())], self.hand)
        if phase == "load":
            return local(self.hand, bufs["all"].at[self.gathered(())])
        if phase == "out":
            mine, dst = bufs["all"], self.dst(me.bit(0))
            return remote(mine, dst, 0) + local(mine, dst)
        if isinstance(phase, tuple):
            done = self.back[: self.back.index(phase[1])]
            part = bufs["all"].at[self.gathered(done)]
            return remote(part, part, phase[1])
        if step > 0:
            done = self.order[: self.order.index(phase)]
            return remote(bufs["acc"].at[self.place(done, phase)], bufs[phase], phase)
        every = (slice(None),) * self.splits
        if phase == "x":
            return remote(self.src(1 - me.shard, every), bufs["x"], "x") + local(
                self.src(me.shard, every), bufs["acc"]
            )
        out = []
        for s in range(2):
            at = lambda bit: tuple(
                bit if k == phase else slice(None) for k in range(1, self.splits + 1)
            )
            out += remote(self.src(s, at(1 - me.bit(phase))), bufs[phase].at[s], phase)
            out += local(self.src(s, at(me.bit(phase))), bufs["acc"].at[s])
        return out

    def then(self, step):
        phase, bufs = self.phases[step], self.bufs
        if phase in self.order:
            at = self.place(self.order[: self.order.index(phase) + 1])
            if phase == self.order[-1]:
                add_into(bufs["acc"], at, bufs[phase], bufs["all"], self.gathered(()))
            else:
                add_into(bufs["acc"], at, bufs[phase])

    def cost(self, step):
        phase = self.phases[step]
        piece = 2 * 2 * int(np.prod(self.shape)) / 1e6
        if phase == "out":
            return [("core", 2**self.splits * piece / 2 / 0.2)]
        if phase in ("store", "load"):
            return [("local" + self.name, 0.5)]
        if isinstance(phase, tuple):
            key = phase[1]
            pieces = 2 ** self.back.index(key)
        else:
            key = phase
            free = [k for k in self.order[self.order.index(key) + 1 :] if k in self.keys]
            pieces = 2 ** len(free)
        busy = pieces * piece / RATE
        if key == 3:
            return [(3, 2 * busy), (2, busy)]
        return [(key, busy)]


def add_into(acc, at, other, out=None, to=None):
    shape = other.shape
    rows = shape[-2]
    block = 48 if rows % 48 == 0 else 32
    lead = int(np.prod(shape[:-2], dtype=int))
    out, to = (acc, at) if out is None else (out, to)

    def fill(index, loop):
        loop = iter(loop)
        return tuple(next(loop) if isinstance(k, slice) else k for k in index)

    def step(i, _):
        place, low = i // (rows // block), (i % (rows // block)) * block
        loop = []
        for size in reversed(shape[:-2]):
            loop.insert(0, place % size)
            place = place // size
        last = (pl.ds(pl.multiple_of(low, block), block), slice(None))
        total = acc[fill(at, loop) + last] + other[tuple(loop) + last]
        out[fill(to, loop) + last] = total
        return 0

    lax.fori_loop(0, lead * (rows // block), step, 0)


def timeline(chains):
    free, events = {}, []
    ready = [(0.0, k, 0) for k in range(len(chains))]
    while ready:
        ready.sort()
        now, k, step = ready.pop(0)
        links = chains[k].cost(step)
        begin = max([now] + [free.get(link, 0.0) for link, _ in links])
        for link, busy in links:
            free[link] = begin + busy
        end = begin + max(busy for _, busy in links) + HOP
        events.append((max(now, begin - 2.0), len(events), "start", chains[k], step))
        events.append((end, len(events), "finish", chains[k], step))
        if step + 1 < len(chains[k].phases):
            ready.append((end, k, step + 1))
    return sorted(events, key=lambda e: (e[0], e[2] == "start", e[1]))


def run(events):
    for _, _, what, one, step in events:
        if what == "start":
            one.start(step)
        else:
            one.finish(step)


def by_tick(events, ticks, length):
    out = [[] for _ in range(ticks)]
    for event in events:
        out[min(int(np.ceil(event[0] / length)), ticks - 1)].append(event)
    return out


def run_tick(now, ticks):
    for at, events in enumerate(ticks):
        if events:

            @pl.when(now == at)
            def _():
                run(events)


def rep_bits():
    return lax.axis_size("rep").bit_length() - 1


def conv_at(buf, prm_ref, lanes, masks):
    taps = [buf[8 : 8 + Q, lanes]]
    for back in (1, 2, 3):
        taps.append(buf[8 - back : 8 - back + Q, lanes] * masks[back - 1])
    conv = prm_ref[4:5, lanes]
    for back in range(4):
        conv = conv + prm_ref[3 - back : 4 - back, lanes] * taps[back]
    return conv, taps


def halves(v):
    low = iota(v.shape, 1) < HEADDIM
    zero = jnp.zeros_like(v)
    return jnp.concatenate([jnp.where(low, v, zero), jnp.where(low, zero, v)], axis=0)


FWD_TICKS = 4


def fwd_kernel(
    xd_ref, segc_ref, segr_ref, cum3_ref, ex_ref, cumt_ref, prm_ref, ind_ref, ind2_ref,
    wt_ref, wo_ref,
    y_ref, sin_ref, conv_ref, wz_oth, wo_oth, buf, state, score, sems_ref,
):
    c = pl.program_id(0)
    chunks = pl.num_programs(0)
    me = Place()
    sems = SemPool(sems_ref)
    parts = []
    for k in range(3):
        order = (1, 2) if k % 2 else (2, 1)
        parts.append(
            Rows(
                me, sems, "z%d" % k,
                lambda piece, k=k: wt_ref.at[pl.ds(piece * 384 + k * 128, 128), :],
                wz_oth, k * 128, 128, order,
            )
        )
        parts.append(
            Rows(
                me, sems, "o%d" % k,
                lambda piece, k=k: wo_ref.at[pl.ds(piece * 192 + k * 64, 64), :],
                wo_oth, k * 64, 64, order[::-1],
            )
        )
    ticks = by_tick(timeline(parts), 8 * FWD_TICKS, 8.0 / FWD_TICKS)
    ending = ticks[-1]
    ticks[-1] = []

    @pl.when(c == 0)
    def _():
        me.greet(("x", 0, 1, 2))

    @pl.when(c == 0)
    def _():
        buf[0:8, :] = jnp.zeros((8, CW), F32)
        state[...] = jnp.zeros_like(state)

    @pl.when(c > 0)
    def _():
        buf[0:8, :] = buf[Q : Q + 8, :]

    buf[8:, :] = xd_ref[:, :CW]
    masks = [segc_ref[:, k : k + 1] for k in (1, 2, 3)]
    conv_bc, _ = conv_at(buf, prm_ref, slice(DI, CW), masks)
    conv_ref[:, DI:] = conv_bc
    bc = conv_bc * sigmoid(conv_bc)
    b_t = bc[:, :N].T.astype(BF)
    b_low = bc[:, :N].astype(BF)
    c_low = bc[:, N:].astype(BF)
    g = dot_nt(c_low, b_low)
    seen = (iota((Q, Q), 0) >= iota((Q, Q), 1)) & (segc_ref[:, 0:1] == segr_ref[0, 0:1, :])
    g = jnp.where(seen, g, 0.0)
    score[...] = jnp.concatenate([g, g], axis=1)

    def group(at, _):
        lanes = pl.ds(pl.multiple_of(at * GW, GW), GW)
        conv, _ = conv_at(buf, prm_ref, lanes, masks)
        conv_ref[:, lanes] = conv
        x = conv * sigmoid(conv)
        spread = dot(ex_ref[0], ind_ref[:, lanes])
        grown = spread[Q : 2 * Q]
        scaled = x * spread[:Q]
        now = state[:, lanes]
        now_low = now.astype(BF)
        sin_ref[0, :, lanes] = now_low
        y = dot(c_low, now_low) * grown + prm_ref[5:6, lanes] * x
        state[:, lanes] = grown[Q - 1 : Q, :] * now + dot(
            b_t, (scaled * spread[2 * Q :]).astype(BF)
        )
        parts = []
        for pair in range(2):
            wide = pl.ds(pl.multiple_of(at * 512 + pair * 256, 256), 256)
            column = dot(cum3_ref[...], ind2_ref[:, wide])
            head = at * 4 + pair * 2
            row = jnp.concatenate(
                [cumt_ref[0, pl.ds(head, 1), :], cumt_ref[0, pl.ds(head + 1, 1), :]], axis=1
            )
            mixed = jnp.exp(jnp.minimum(column - row, 0.0)) * score[...]
            values = halves(scaled[:, pair * 128 : (pair + 1) * 128]).astype(BF)
            parts.append(dot(mixed.astype(BF), values))
        y_ref[:, lanes] = y + jnp.concatenate(parts, axis=1)
        return 0

    def groups(place, _):
        run_tick(c * FWD_TICKS + place, ticks)
        for k in range(DI // GW // FWD_TICKS):
            group(place * (DI // GW // FWD_TICKS) + k, 0)
        return 0

    lax.fori_loop(0, FWD_TICKS, groups, 0)

    @pl.when(c == chunks - 1)
    def _():
        run(ending)


def scan_fwd(xd, segc, segr, cum3, ex, cumt, prm, ind, ind2, w_t, wo):
    hbm = pl.BlockSpec(memory_space=pl.ANY)
    tokens = xd.shape[0]
    chunks = tokens // Q
    fixed = lambda c: (0, 0)
    return pl.pallas_call(
        fwd_kernel,
        grid=(chunks,),
        in_specs=[
            pl.BlockSpec((Q, XD), lambda c: (c, 0)),
            pl.BlockSpec((Q, 16), lambda c: (c, 0)),
            pl.BlockSpec((1, 8, Q), lambda c: (c, 0, 0)),
            pl.BlockSpec((Q, 256), lambda c: (c, 0)),
            pl.BlockSpec((1, 3 * Q, 128), lambda c: (c, 0, 0)),
            pl.BlockSpec((1, H, Q), lambda c: (c, 0, 0)),
            pl.BlockSpec((8, XD), fixed),
            pl.BlockSpec((128, DI), fixed),
            pl.BlockSpec((256, H * Q), fixed),
            hbm,
            hbm,
        ],
        out_specs=[
            pl.BlockSpec((Q, DI), lambda c: (c, 0)),
            pl.BlockSpec((1, N, DI), lambda c: (c, 0, 0)),
            pl.BlockSpec((Q, CW), lambda c: (c, 0)),
            hbm,
            hbm,
        ],
        out_shape=[
            jax.ShapeDtypeStruct((tokens, DI), F32),
            jax.ShapeDtypeStruct((chunks, N, DI), BF),
            jax.ShapeDtypeStruct((tokens, CW), F32),
            jax.ShapeDtypeStruct((2, 2, 2, 384, D // 2), BF),
            jax.ShapeDtypeStruct((2, 2, 2, 192, D), BF),
        ],
        scratch_shapes=[
            pltpu.VMEM((Q + 8, CW), F32),
            pltpu.VMEM((N, DI), F32),
            pltpu.VMEM((Q, 2 * Q), F32),
            pltpu.SemaphoreType.DMA((320,)),
        ],
        compiler_params=pltpu.CompilerParams(
            dimension_semantics=("arbitrary",), collective_id=3, has_side_effects=True,
            vmem_limit_bytes=60 << 20,
        ),
        cost_estimate=pl.CostEstimate(
            flops=20_000_000_000, bytes_accessed=38_000_000, transcendentals=12_000_000
        ),
        name="scan_fwd",
    )(xd, segc, segr, cum3, ex, cumt, prm, ind, ind2, w_t, wo)


GT = 512


def owner_lanes(index, low, size, width):
    return pl.ds(pl.multiple_of(index * width + low, 128), size)


def gate_kernel(
    y_ref, nrm_ref, g_ref, u_ref, wz_own, wz_oth, wo_own, wo_oth, gain_ref,
    gn2_ref, dz2_ref, dz_ref, dy_ref, bo_ref, gg_ref, zs, dg, gn_held, dz_held, sems,
):
    rows = y_ref.shape[0]
    me = Place()
    shard = me.shard
    block, blocks = pl.program_id(0), pl.num_programs(0)
    half = DI // 2

    @pl.when(block == 0)
    def _():
        gg_ref[...] = jnp.zeros_like(gg_ref)
        me.greet((0,))

    def sent(block):
        remote, local = copiers(me, sems, block * 16, 16)
        slot = block % 2
        to = pl.ds(pl.multiple_of(block * rows, rows), rows)
        out = []
        for core, move in ((me.bit(0), None), (1 - me.bit(0), 0)):
            pairs = [(dz_held.at[slot, :, owner_lanes(core, 0, half, half)], dz2_ref, 0, half)]
            for s in range(2):
                low = s * half
                lanes = pl.ds(pl.multiple_of(core * (half // 2) + low, 128), half // 2)
                pairs.append((gn_held.at[slot, :, lanes], gn2_ref, s * (half // 2), half // 2))
            for src, both, low, width in pairs:
                if move is None:
                    out += local(src, both.at[0, to, pl.ds(low, width)])
                else:
                    dst = both.at[1, to, pl.ds(low, width)]
                    out += remote(src, dst, move)
        return out + local(dz_held.at[slot], dz_ref.at[to, :])

    @pl.when(block >= 2)
    def _():
        for copy in sent(block - 2):
            copy.wait()

    slot = block % 2

    def fold(v):
        return sum(v[:, k * 128 : (k + 1) * 128] for k in range(v.shape[1] // 128))

    nrm_own = owner_lanes(shard, 0, D // 2, D // 2)
    nrm_oth = owner_lanes(1 - shard, 0, D // 2, D // 2)
    squares = jnp.zeros((rows, 128), F32)
    moments = jnp.zeros((rows, 128), F32)
    for owner, wo in ((shard, wo_own), (1 - shard, wo_oth)):
        for at in range(DI // 2 // GT):
            lanes = owner_lanes(owner, at * GT, GT, DI // 2)
            z = dot_nt(nrm_ref[0, :, nrm_own], wz_own[lanes, :])
            z += dot_nt(nrm_ref[0, :, nrm_oth], wz_oth[lanes, :])
            d = dot_nt(g_ref[...], wo[at * GT : (at + 1) * GT, :]) * gain_ref[:, lanes]
            gated = y_ref[:, lanes] * (z * sigmoid(z))
            zs[:, lanes] = z
            dg[:, lanes] = d
            squares += fold(gated * gated)
            moments += fold(gated * d)
    r = lax.rsqrt(jnp.sum(squares, axis=1, keepdims=True) * (1.0 / DI) + EPS)
    k = r * r * r * (jnp.sum(moments, axis=1, keepdims=True) * (1.0 / DI))
    for at in range(DI // GT):
        lanes = slice(at * GT, (at + 1) * GT)
        z = zs[:, lanes]
        d = dg[:, lanes]
        y = y_ref[:, lanes]
        gain = gain_ref[:, lanes]
        sig = sigmoid(z)
        silu = z * sig
        gated = y * silu
        normal = gated * r
        gn_held[slot, :, lanes] = (normal * gain).astype(BF)
        d_gated = r * d - gated * k
        dy_ref[:, lanes] = (d_gated * silu).astype(BF)
        dz_held[slot, :, lanes] = (d_gated * y * (sig + silu * (1.0 - sig))).astype(BF)
        gg_ref[0:1, lanes] += jnp.sum(d * normal, axis=0, keepdims=True) / gain
    for copy in sent(block):
        copy.start()
    out = u_ref[...].astype(F32)
    for owner, wo in ((shard, wo_own), (1 - shard, wo_oth)):
        out += dot(gn_held[slot, :, owner_lanes(owner, 0, half, half)], wo[...])
    bo_ref[...] = out.astype(BF)

    @pl.when(block == blocks - 1)
    def _():
        for copy in sent(block - 1) + sent(block):
            copy.wait()


def gate(y, nrm, g, u, w_t, wz_oth, wo_own, wo_oth, gain):
    tokens = y.shape[0]
    rows = 256
    by_row = lambda i: (i, 0)
    fixed = lambda i: (0, 0)
    hbm = pl.BlockSpec(memory_space=pl.ANY)
    once = dict(pipeline_mode=pl.Buffered(1))
    return pl.pallas_call(
        gate_kernel,
        grid=(tokens // rows,),
        in_specs=[
            pl.BlockSpec((rows, DI), by_row),
            pl.BlockSpec((1, rows, D), lambda i: (0, i, 0)),
            pl.BlockSpec((rows, D), by_row),
            pl.BlockSpec((rows, D), by_row),
            pl.BlockSpec((DI, D // 2), fixed, **once),
            pl.BlockSpec((DI, D // 2), fixed, **once),
            pl.BlockSpec((DI // 2, D), fixed, **once),
            pl.BlockSpec((DI // 2, D), fixed, **once),
            pl.BlockSpec((1, DI), fixed),
        ],
        out_specs=[
            hbm,
            hbm,
            hbm,
            pl.BlockSpec((rows, DI), by_row),
            pl.BlockSpec((rows, D), by_row),
            pl.BlockSpec((8, DI), fixed),
        ],
        out_shape=[
            jax.ShapeDtypeStruct((2, tokens, DI // 2), BF),
            jax.ShapeDtypeStruct((2, tokens, DI // 2), BF),
            jax.ShapeDtypeStruct((tokens, DI), BF),
            jax.ShapeDtypeStruct((tokens, DI), BF),
            jax.ShapeDtypeStruct((tokens, D), BF),
            jax.ShapeDtypeStruct((8, DI), F32),
        ],
        scratch_shapes=[
            pltpu.VMEM((rows, DI), F32),
            pltpu.VMEM((rows, DI), F32),
            pltpu.VMEM((2, rows, DI), BF),
            pltpu.VMEM((2, rows, DI), BF),
            pltpu.SemaphoreType.DMA((16 * (tokens // rows),)),
        ],
        compiler_params=pltpu.CompilerParams(
            dimension_semantics=("arbitrary",), collective_id=4, has_side_effects=True,
            vmem_limit_bytes=60 << 20,
        ),
        cost_estimate=pl.CostEstimate(
            flops=29_000_000_000, bytes_accessed=64_000_000, transcendentals=6_000_000
        ),
        name="gate",
    )(y, nrm, g, u, w_t, wz_oth, wo_own, wo_oth, gain)


def widen_kernel(gz0_ref, gz1_ref, gx_ref, gb_ref, go0_ref, go1_ref, inner_ref, outer_ref):
    at = pl.program_id(0)
    first, outer_first = to_end("gz") // 2, to_end("go")

    def fill(when, out, ref):
        @pl.when(when)
        def _():
            out[...] = ref[...].astype(F32)

    fill((at < 4) & (at % 2 < first), inner_ref, gz0_ref)
    fill((at < 4) & (at % 2 >= first), inner_ref, gz1_ref)
    fill((at >= 4) & (at < 8), inner_ref, gx_ref)
    fill((at < 6) & (at % 3 < outer_first), outer_ref, go0_ref)
    fill((at < 6) & (at % 3 >= outer_first), outer_ref, go1_ref)

    @pl.when(at == 8)
    def _():
        inner_ref[:384, :] = gb_ref[...].astype(F32)


def widen(gz0, gz1, gx, gb, go0, go1):
    half = D // 2

    def rows(height, cols, low, high, each, base=0):
        def at(i):
            i = jnp.clip(i - base, 0, 2 * each - 1)
            return ((i // each) * (high - low) + jnp.clip(i % each - low, 0, high - low - 1), 0)

        return pl.BlockSpec((height, cols), at)

    first, outer_first = to_end("gz") // 2, to_end("go")
    assert to_end("gz") == 2
    return pl.pallas_call(
        widen_kernel,
        grid=(9,),
        in_specs=[
            rows(768, half, 0, first, 2), rows(768, half, first, 2, 2), rows(768, half, 0, 2, 2, 4),
            pl.BlockSpec((384, half), lambda i: (0, 0)),
            rows(256, D, 0, outer_first, 3), rows(256, D, outer_first, 3, 3),
        ],
        out_specs=[
            pl.BlockSpec((768, half), lambda i: (i, 0)),
            pl.BlockSpec((256, D), lambda i: (jnp.minimum(i, 5), 0)),
        ],
        out_shape=[
            jax.ShapeDtypeStruct((CW + DI + H, half), F32),
            jax.ShapeDtypeStruct((DI // 2, D), F32),
        ],
        compiler_params=params(60),
        cost_estimate=pl.CostEstimate(flops=0, bytes_accessed=44_000_000, transcendentals=0),
        name="widen",
    )(
        gz0.reshape(-1, half), gz1.reshape(-1, half), gx.reshape(-1, half), gb.reshape(-1, half),
        go0.reshape(-1, D), go1.reshape(-1, D),
    )


BWD_TICKS = 4


def bwd_kernel(
    bits,
    xd_ref, conv_ref, dy_ref, sin_ref, segc_ref, segr_ref, cum3_ref, ex_ref, cumt_ref, prm_ref,
    ind_ref, ind2_ref, ind_t_ref, rho_t_ref, go, gz,
    dxd_ref, dx2_ref, pg_ref, go_hand, gz_hand, go_out, gz_out,
    dbuf, dstate, score, d_score, d_b, d_c, rho, red, gam, kept, held, pair_sems, *rest,
):
    c = pl.program_id(0)
    chunks = pl.num_programs(0)
    me = Place()
    slot = c % 2

    def sent(c):
        remote, local = copiers(me, pair_sems, c * 12, 12)
        mine = held.at[c % 2]
        to = pl.ds(pl.multiple_of((chunks - 1 - c) * Q, Q), Q)
        lanes = lambda core: owner_lanes(core, 0, DI // 2, DI // 2)
        tail = mine.at[:, pl.ds(DI, XD - DI)]
        half, rest = pl.ds(0, DI // 2), pl.ds(DI // 2, XD - DI)
        return (
            remote(mine.at[:, lanes(1 - me.bit(0))], dx2_ref.at[1, to, half], 0)
            + remote(tail, dx2_ref.at[1, to, rest], 0)
            + local(mine.at[:, lanes(me.bit(0))], dx2_ref.at[0, to, half])
            + local(tail, dx2_ref.at[0, to, rest])
            + local(mine, dxd_ref.at[to, :])
        )

    @pl.when(c >= 2)
    def _():
        for copy in sent(c - 2):
            copy.wait()

    items = plan_items(
        me, SemPool(rest[-1]), list(rest[:-1]), early_plan(), dict(go=go, gz=gz),
        dict(go=(go_out, 0), gz=(gz_out, 0)), dict(go=go_hand, gz=gz_hand),
    )
    ticks = by_tick(timeline(items), 8 * BWD_TICKS, 14.4 / BWD_TICKS)
    ending = ticks[-1]
    ticks[-1] = []

    @pl.when(c == 0)
    def _():
        me.greet(("x",) + tuple(range(bits)))

    @pl.when(c == 0)
    def _():
        dbuf[Q:, :] = jnp.zeros((8, CW), F32)
        dstate[...] = jnp.zeros_like(dstate)
        pg_ref[...] = jnp.zeros_like(pg_ref)

    @pl.when(c > 0)
    def _():
        dbuf[Q:, :] = dbuf[0:8, :]

    masks_next = [segc_ref[:, k : k + 1] for k in (6, 7, 8)]

    def conv_back(lanes, d_conv):
        dbuf[0:Q, lanes] = d_conv
        raw = xd_ref[:, lanes]
        moved = d_conv
        total = 0.0
        for ahead in range(4):
            if ahead:
                moved = dbuf[ahead : ahead + Q, lanes] * masks_next[ahead - 1]
            total += prm_ref[3 - ahead : 4 - ahead, lanes] * moved
            pg_ref[3 - ahead : 4 - ahead, lanes] += jnp.sum(moved * raw, axis=0, keepdims=True)
        held[slot, :, lanes] = total.astype(BF)
        pg_ref[4:5, lanes] += jnp.sum(d_conv, axis=0, keepdims=True)

    conv_bc = conv_ref[:, DI:]
    sig_bc = sigmoid(conv_bc)
    bc = conv_bc * sig_bc
    c_t = bc[:, N:].T.astype(BF)
    b_low = bc[:, :N].astype(BF)
    c_low = bc[:, N:].astype(BF)
    g = dot_nt(b_low, c_low)
    seen = (iota((Q, Q), 0) <= iota((Q, Q), 1)) & (segc_ref[:, 0:1] == segr_ref[0, 0:1, :])
    g = jnp.where(seen, g, 0.0)
    score[...] = jnp.concatenate([g, g], axis=1)
    d_score[...] = jnp.zeros_like(d_score)
    d_b[...] = jnp.zeros_like(d_b)
    d_c[...] = jnp.zeros_like(d_c)
    rho[...] = jnp.zeros_like(rho)
    red[...] = jnp.zeros_like(red)

    def group(at, _):
        lanes = pl.ds(pl.multiple_of(at * GW, GW), GW)
        conv = conv_ref[:, lanes]
        sig = sigmoid(conv)
        x = conv * sig
        spread = dot(ex_ref[0], ind_ref[:, lanes])
        step = spread[:Q]
        grown = spread[Q : 2 * Q]
        to_end = spread[2 * Q :]
        scaled = x * step
        dy_low = dy_ref[:, lanes]
        dy = dy_low.astype(F32)
        dy_grown = (dy * grown).astype(BF)
        s_in = sin_ref[0, :, lanes]
        ds = dstate[:, lanes]
        ds_low = ds.astype(BF)
        carried = dy * (dot(c_low, s_in) * grown)
        d_left = dot(b_low, ds_low) * to_end
        leaving = scaled * d_left
        d_c[...] += dot_nt(dy_grown, s_in)
        d_b[...] += dot_nt((scaled * to_end).astype(BF), ds_low)
        kept_row = grown[Q - 1 : Q, :]
        kept[0:1, lanes] = kept_row * jnp.sum(s_in.astype(F32) * ds, axis=0, keepdims=True)
        dstate[:, lanes] = kept_row * ds + dot(c_t, dy_grown)
        parts = []
        for pair in range(2):
            own = slice(pair * 128, (pair + 1) * 128)
            wide = pl.ds(pl.multiple_of(at * 512 + pair * 256, 256), 256)
            column = dot(cum3_ref[...], ind2_ref[:, wide])
            head = at * 4 + pair * 2
            row = jnp.concatenate(
                [cumt_ref[0, pl.ds(head, 1), :], cumt_ref[0, pl.ds(head + 1, 1), :]], axis=1
            )
            decay = jnp.exp(jnp.minimum(row - column, 0.0))
            values = halves(dy_low[:, own])
            d_mixed = dot_nt(scaled[:, own].astype(BF), values) * decay
            d_score[...] += d_mixed[:, :Q] + d_mixed[:, Q:]
            through = score[...]
            parts.append(dot((decay * through).astype(BF), values))
            change = (d_mixed * through).astype(BF)
            rho[...] += dot(change, rho_t_ref[wide, :])
            sums = jnp.sum(change.astype(F32), axis=0, keepdims=True)
            gam[pl.ds(head, 1), :] = sums[:, :Q]
            gam[pl.ds(head + 1, 1), :] = sums[:, Q:]
        d_scaled = jnp.concatenate(parts, axis=1) + d_left
        red[...] += dot(
            jnp.concatenate([carried, leaving, d_scaled * x], axis=0).astype(BF),
            ind_t_ref[lanes, :],
        )
        pg_ref[5:6, lanes] += jnp.sum(dy * x, axis=0, keepdims=True)
        d_x = d_scaled * step + prm_ref[5:6, lanes] * dy
        conv_back(lanes, d_x * (sig + x * (1.0 - sig)))
        return 0

    def groups(place, _):
        run_tick(c * BWD_TICKS + place, ticks)
        for k in range(DI // GW // BWD_TICKS):
            group(place * (DI // GW // BWD_TICKS) + k, 0)
        return 0

    lax.fori_loop(0, BWD_TICKS, groups, 0)

    d_score[...] = jnp.where(seen, d_score[...], 0.0)
    ds_low = d_score[...].astype(BF)
    d_b_all = d_b[...] + dot(ds_low, c_low)
    d_c_all = d_c[...] + dot(d_score[...].T.astype(BF), b_low)
    d_bc = jnp.concatenate([d_b_all, d_c_all], axis=1)
    conv_back(slice(DI, CW), d_bc * (sig_bc + bc * (1.0 - sig_bc)))

    kept_all = jnp.broadcast_to(kept[0:1, :], (16, DI))
    kept_high = kept_all.astype(BF)
    kept_low = (kept_all - kept_high.astype(F32)).astype(BF)
    kept_sum = (dot(kept_high, ind_t_ref[...]) + dot(kept_low, ind_t_ref[...]))[0:1, :]
    gam_t = jnp.concatenate([gam[...], jnp.zeros((128 - H, Q), F32)], axis=0).T
    after = (iota((Q, Q), 0) <= iota((Q, Q), 1)).astype(F32)
    before = (iota((Q, Q), 0) > iota((Q, Q), 1)).astype(F32)
    d_log = (
        jnp.dot(after, red[0:Q, :] + gam_t - rho[...], precision=HIGH, preferred_element_type=F32)
        + jnp.dot(before, red[Q : 2 * Q, :], precision=HIGH, preferred_element_type=F32)
        + kept_sum
    )
    head = iota((Q, 128), 1) < H
    value = xd_ref[:, CW:] + prm_ref[6:7, :128]
    rate = -jnp.exp(prm_ref[7:8, :128])
    d_raw = jnp.where(head, (red[2 * Q :, :] + d_log * rate) * sigmoid(value), 0.0)
    held[slot, :, CW:] = d_raw.astype(BF)
    for copy in sent(c):
        copy.start()
    pg_ref[6:7, :128] += jnp.sum(d_raw, axis=0, keepdims=True)
    pg_ref[7:8, :128] += jnp.sum(
        jnp.where(head, d_log * rate * softplus(value), 0.0), axis=0, keepdims=True
    )

    @pl.when(c == chunks - 1)
    def _():
        run(ending)
        for copy in sent(c - 1) + sent(c):
            copy.wait()


def scan_bwd(xd, conv, dy, sin, segc, segr, cum3, ex, cumt, prm, ind, ind2, ind_t, rho_t, go, gz):
    tokens = xd.shape[0]
    bits = rep_bits()
    hbm = pl.BlockSpec(memory_space=pl.ANY)
    chunks = tokens // Q
    fixed = lambda c: (0, 0)
    back = lambda c: (chunks - 1 - c, 0)
    back3 = lambda c: (chunks - 1 - c, 0, 0)
    once = dict(pipeline_mode=pl.Buffered(1))
    return pl.pallas_call(
        functools.partial(bwd_kernel, bits),
        grid=(chunks,),
        in_specs=[
            pl.BlockSpec((Q, XD), back),
            pl.BlockSpec((Q, CW), back),
            pl.BlockSpec((Q, DI), back),
            pl.BlockSpec((1, N, DI), back3),
            pl.BlockSpec((Q, 16), back),
            pl.BlockSpec((1, 8, Q), back3),
            pl.BlockSpec((Q, 256), back),
            pl.BlockSpec((1, 3 * Q, 128), back3),
            pl.BlockSpec((1, H, Q), back3),
            pl.BlockSpec((8, XD), fixed),
            pl.BlockSpec((128, DI), fixed, **once),
            pl.BlockSpec((256, H * Q), fixed, **once),
            pl.BlockSpec((DI, 128), fixed, **once),
            pl.BlockSpec((H * Q, 128), fixed, **once),
            hbm,
            hbm,
        ],
        out_specs=[hbm] * 2 + [pl.BlockSpec((8, XD), fixed)] + [hbm] * 4,
        out_shape=[
            jax.ShapeDtypeStruct((tokens, XD), BF),
            jax.ShapeDtypeStruct((2, tokens, XD - DI // 2), BF),
            jax.ShapeDtypeStruct((8, XD), F32),
            part_array("go", 3 - to_end("go"), sent=True),
            part_array("gz", 4 - to_end("gz"), sent=True),
            part_array("go", to_end("go")),
            part_array("gz", to_end("gz")),
        ],
        scratch_shapes=[
            pltpu.VMEM((Q + 8, CW), F32),
            pltpu.VMEM((N, DI), F32),
            pltpu.VMEM((Q, 2 * Q), F32),
            pltpu.VMEM((Q, Q), F32),
            pltpu.VMEM((Q, N), F32),
            pltpu.VMEM((Q, N), F32),
            pltpu.VMEM((Q, 128), F32),
            pltpu.VMEM((3 * Q, 128), F32),
            pltpu.VMEM((H, Q), F32),
            pltpu.VMEM((8, DI), F32),
            pltpu.VMEM((2, Q, XD), BF),
            pltpu.SemaphoreType.DMA((12 * chunks,)),
            *plan_scratch(bits, early_plan()),
            pltpu.SemaphoreType.DMA((1024,)),
        ],
        compiler_params=pltpu.CompilerParams(
            dimension_semantics=("arbitrary",), collective_id=1, has_side_effects=True,
            vmem_limit_bytes=60 << 20,
        ),
        cost_estimate=pl.CostEstimate(
            flops=60_000_000_000, bytes_accessed=50_000_000, transcendentals=18_000_000
        ),
        name="scan_bwd",
    )(
        xd, conv, dy, sin, segc, segr, cum3, ex, cumt, prm, ind, ind2, ind_t, rho_t,
        in_parts("go", go), in_parts("gz", gz),
    )


def gather_kernel(
    u_ref, vec_ref, wt_ref, wb_ref, g_ref,
    wx_oth, wb_oth, vec2_ref, nrm2_ref, g2_ref, raw_ref, xd_ref,
    gain, weights, arrived, acc, nrm_ref, g_held, sems_ref,
):
    me = Place()
    s = me.shard
    sems = SemPool(sems_ref)
    tokens = u_ref.shape[0]
    half = D // 2
    own = pl.ds(pl.multiple_of(s * half, half), half)
    oth = pl.ds(pl.multiple_of((1 - s) * half, half), half)
    parts = []
    for k, order in enumerate(((1, 2), (2, 1), (1, 2))):
        parts.append(
            Rows(
                me, sems, "x%d" % k,
                lambda piece, k=k: wt_ref.at[pl.ds(DI + piece * 384 + k * 128, 128), :],
                wx_oth, k * 128, 128, order,
            )
        )
    parts.append(
        Rows(
            me, sems, "b", lambda piece: wb_ref.at[pl.ds(piece * 48, 48), :], wb_oth, 0, 48, (2, 1)
        )
    )
    at = sems.reserve(24)
    pairs = sems.reserve(16)
    me.greet(("x", 0, 1, 2))
    swap = pltpu.make_async_remote_copy(
        vec_ref, vec2_ref.at[s], sems_ref.at[at], sems_ref.at[at + 1], device_id=me.partner("x"),
        device_id_type=pl.DeviceIdType.MESH,
    )
    swap.start()
    for part in parts:
        part.start(0)
    loads = [
        (vec_ref, vec2_ref.at[s]),
        (wt_ref.at[pl.ds(DI, DI), :], weights.at[pl.ds(0, DI), :]),
        (wb_ref, weights.at[pl.ds(DI, 384), :]),
    ]
    loads = [pltpu.make_async_copy(*v, sems_ref.at[at + 2 + k]) for k, v in enumerate(loads)]
    for copy in loads:
        copy.start()
    fetch = pltpu.make_async_copy(g_ref, g_held, sems_ref.at[pairs])
    fetch.start()

    def share(held, both, base):
        remote, local = copiers(me, sems_ref, base, 5)
        return remote(held, both.at[1], 0) + local(held, both.at[0])

    swap.wait()
    loads[0].wait()
    fetch.wait()
    shared = share(g_held, g2_ref, pairs + 1)
    for copy in shared:
        copy.start()
    for shard in range(2):
        for k in range(half // 128):
            low = shard * half + k * 128
            gain[0:1, low : low + 128] = vec2_ref[shard, k : k + 1, :]

    def norm(at, _):
        rows = pl.ds(pl.multiple_of(at * 128, 128), 128)
        u = u_ref[rows, :].astype(F32)
        q = lax.rsqrt(jnp.sum(u * u, axis=1, keepdims=True) * (1.0 / D) + EPS)
        nrm_ref[rows, :] = (u * q * gain[...]).astype(BF)
        return 0

    lax.fori_loop(0, tokens // 128, norm, 0)
    later = share(nrm_ref, nrm2_ref, pairs + 6)
    for copy in later:
        copy.start()
    loads[1].wait()
    loads[2].wait()

    def by_rows(body):
        body(slice(0, tokens))

    def first(low):
        def body(rows):
            acc[rows, low : low + 384] = dot_nt(nrm_ref[rows, own], weights[low : low + 384, :])

        by_rows(body)

    def arrive(k):
        source = wx_oth.at[:, :, :, pl.ds(k * 128, 128), :]
        return pltpu.make_async_copy(source, arrived.at[k], sems_ref.at[at + 8 + k])

    def second(k, piece):
        if piece == 0:
            arrive(k).wait()
        low = piece * 384 + k * 128

        def body(rows):
            acc[rows, low : low + 128] += dot_nt(
                nrm_ref[rows, oth], arrived[k, piece // 4, (piece // 2) % 2, piece % 2]
            )

        by_rows(body)

    events = [e for e in timeline(parts) if not (e[2] == "start" and e[4] == 0)]
    work = [(1.3, functools.partial(first, low)) for low in range(0, XD, 384)]
    now = 8.0
    while events or work:
        if work and (not events or events[0][0] > now + 0.5):
            long, task = work.pop(0)
            task()
            now += long
            continue
        event = events.pop(0)
        run([event])
        now = max(now, event[0])
        _, _, what, part, step = event
        k = parts.index(part)
        if what == "finish" and step == 3 and k < 3:
            arrive(k).start()
            work += [(0.6, functools.partial(second, k, piece)) for piece in range(8)]
    loads = []
    for k in range(8):
        source = wb_oth.at[k // 4, (k // 2) % 2, k % 2]
        target = weights.at[pl.ds(k * 48, 48), :]
        loads.append(pltpu.make_async_copy(source, target, sems_ref.at[at + 16 + k]))
    for copy in loads:
        copy.start()
    for copy in loads:
        copy.wait()

    def last(at, _):
        rows = pl.ds(pl.multiple_of(at * 256, 256), 256)
        acc[rows, DI:] += dot_nt(nrm_ref[rows, oth], weights[:384, :])
        return 0

    lax.fori_loop(0, tokens // 256, last, 0)
    out = pltpu.make_async_copy(acc, xd_ref, sems_ref.at[at + 13])
    out.start()
    raw_ref[...] = acc[:, CW:]
    for copy in shared + later:
        copy.wait()
    out.wait()


def gather(u, vec, wt, wb, g):
    tokens = u.shape[0]
    vmem = pl.BlockSpec(memory_space=pltpu.VMEM)
    hbm = pl.BlockSpec(memory_space=pl.ANY)
    sds = jax.ShapeDtypeStruct
    return pl.pallas_call(
        gather_kernel,
        in_specs=[vmem, vmem, hbm, hbm, hbm],
        out_specs=[hbm, hbm, vmem, hbm, hbm, vmem, hbm],
        out_shape=[
            sds((2, 2, 2, 384, D // 2), BF),
            sds((2, 2, 2, 48, D // 2), BF),
            sds((2, VEC, 128), F32),
            sds((2, tokens, D), BF),
            sds((2, tokens, D), BF),
            sds((tokens, 128), F32),
            sds((tokens, XD), F32),
        ],
        scratch_shapes=[
            pltpu.VMEM((1, D), F32),
            pltpu.VMEM((XD, D // 2), BF),
            pltpu.VMEM((3, 2, 2, 2, 128, D // 2), BF),
            pltpu.VMEM((tokens, XD), F32),
            pltpu.VMEM((tokens, D), BF),
            pltpu.VMEM((tokens, D), BF),
            pltpu.SemaphoreType.DMA((256,)),
        ],
        compiler_params=pltpu.CompilerParams(
            collective_id=0, has_side_effects=True, vmem_limit_bytes=60 << 20
        ),
        cost_estimate=pl.CostEstimate(
            flops=11_000_000_000, bytes_accessed=40_000_000, transcendentals=1024
        ),
        name="gather",
    )(u, vec, wt, wb, g)


TAIL_ROWS = 256
TAIL_PLACES = 6

EARLY = [
    ("go", 1, (1, 2, "x", 3), (3, 1, 2), False),
    ("gz", 1, ("x", 1, 2, 3), (3, 2, 1), True),
    ("go", 0, ("x", 1, 2, 3), (2, 3, 1), True),
    ("gz", 0, ("x", 1, 2, 3), (2, 3, 1), True),
    ("go", 2, ("x", 1, 2, 3), (3, 1, 2), False),
    ("gz", 2, (2, 1, "x", 3), (3, 2, 1), False),
    ("gz", 3, (2, "x", 1, 3), (1, 2, 3), False),
]
LATE = [
    ("gz", 2, ("x", 1, 2, 3), (2, 3, 1)),
    ("gx", 2, (2, 1, "x", 3), (1, 3, 2)),
    ("gx", 3, ("x", 1, 2, 3), (3, 2, 1)),
    ("gx", 0, ("x", 1, 2, 3), (3, 1, 2)),
    ("gb", 0, ("x", 1, 2, 3), (3, 2, 1)),
    ("gx", 1, (1, "x", 2, 3), (2, 3, 1)),
    ("go", 2, ("x", 1, 2, 3), (3, 2, 1)),
    ("go", 1, ("x", 1, 2, 3), (2, 3, 1)),
    ("gz", 3, (1, "x", 2, 3), (3, 2, 1)),
]
KINDS = dict(
    go=(3, 3, 32, D), gz=(4, 3, 48, D // 2), gx=(4, 3, 48, D // 2), gb=(1, 2, 48, D // 2)
)


def to_end(kind):
    return sum(1 for k, _, _, _, full in EARLY if k == kind and full)


def early_plan():
    return [(k, n, "all" if full else "early", o, back) for k, n, o, back, full in EARLY]


def tail_plan():
    return [
        (k, n, "all" if k in ("gx", "gb") else "late", order, back) for k, n, order, back in LATE
    ]


def plan_scratch(bits, plan):
    out = []
    for kind, _, part, order, _ in plan:
        _, splits, rows, cols = KINDS[kind]
        out += Item.shapes(bits, part, order, splits, (rows, cols))
    return out


def plan_items(me, sems, refs, plan, grads, outs, hands):
    half = D // 2
    items = []
    for kind, n, part, order, back in plan:
        _, splits, rows, cols = KINDS[kind]
        grad, (out, first), hand = grads.get(kind), outs.get(kind, (None, 0)), None
        if part != "all":
            hand = hands[kind].at[n - to_end(kind)]
        if kind == "go":
            src = lambda s, at, grad=grad, n=n: grad.at[(s, n) + at]
        else:
            lead = (n,) if kind != "gb" else (4, me.bit(0))
            src = lambda s, at, grad=grad, lead=lead: grad.at[
                lead + at + (slice(None), pl.ds(pl.multiple_of(s * half, half), half))
            ]
        dst = lambda core, out=out, at=n - first: out.at[core, at]
        items.append(
            Item(
                me, sems, kind + str(n), part, order, back, splits, (rows, cols), refs, src, dst, hand
            )
        )
    return items


def part_array(kind, count, sent=False):
    _, splits, rows, cols = KINDS[kind]
    lead = (count,) if sent else (2, count) + (2,) * splits
    return jax.ShapeDtypeStruct(lead + (rows, cols), BF)


def in_parts(kind, grad):
    parts, splits, rows, _ = KINDS[kind]
    lead = (2, parts) if kind == "go" else (parts,)
    return grad.reshape(lead + (2,) * splits + (rows, D))


def tail_kernel(
    bits,
    dz_ref, dxd_ref, u_ref, g_ref, gain_ref, w_own, wb_own, wz_oth, wx_oth, wb_oth,
    go_hand, gz_hand, gx, small,
    out_ref, gg_out, go_out, gz_out, gx_out, gb_out, small_out,
    wz0, wx0, wb0, wz1, wx1, wb1, gg, dn, sm_send, sm_sum, sm_recv, *rest,
):
    c = pl.program_id(0)
    steps = pl.num_programs(0)
    rest, sem_ref = list(rest[:-1]), rest[-1]
    me = Place()
    sems = SemPool(sem_ref)
    half = D // 2
    loads = [
        (w_own.at[pl.ds(0, DI), :], wz0), (w_own.at[pl.ds(DI, DI), :], wx0), (wb_own, wb0),
        (wz_oth, wz1), (wx_oth, wx1), (wb_oth, wb1),
    ]
    load_base = sems.reserve(len(loads))

    def load(k):
        return pltpu.make_async_copy(*loads[k], sem_ref.at[load_base + k])

    items = plan_items(
        me, sems, rest, tail_plan(), dict(gx=gx, gb=gx),
        dict(go=(go_out, to_end("go")), gz=(gz_out, to_end("gz")), gx=(gx_out, 0), gb=(gb_out, 0)),
        dict(go=go_hand, gz=gz_hand),
    )
    ticks = by_tick(timeline(items), 4 * TAIL_PLACES, 10.4 / TAIL_PLACES)
    ending = ticks[-1]
    ticks[-1] = []

    @pl.when(c == 0)
    def _():
        gg[...] = jnp.zeros_like(gg)
        me.greet(("x",) + tuple(range(bits)))
        for k in range(len(loads)):
            load(k).start()

    shard = me.shard
    place = 0
    for part, (owner, wz, wx, wb) in enumerate(
        [(shard, wz0, wx0, wb0), (1 - shard, wz1, wx1, wb1)]
    ):
        for low in range(0, half, 256):
            run_tick(c * TAIL_PLACES + place, ticks)
            place += 1
            if low == 0:

                @pl.when(c == 0)
                def _():
                    for k in range(3 * part, 3 * part + 3):
                        load(k).wait()

            lanes = owner_lanes(owner, low, 256, half)
            own = slice(low, low + 256)
            total = dot(dz_ref[...], wz[:, own]) + dot(dxd_ref[:, :DI], wx[:, own])
            dn[:, lanes] = total + dot(dxd_ref[:, DI:], wb[:, own])
    u = u_ref[...].astype(F32)
    d = dn[...]
    q = lax.rsqrt(jnp.sum(u * u, axis=1, keepdims=True) * (1.0 / D) + EPS)
    scaled = d * gain_ref[...]
    mean = jnp.sum(scaled * u, axis=1, keepdims=True) * (1.0 / D)
    out_ref[...] = g_ref[...].astype(F32) + q * scaled - u * (q * q * q * mean)
    gg[0:1, :] += jnp.sum(d * u * q, axis=0, keepdims=True)

    @pl.when(c == steps - 1)
    def _():
        base = sems.reserve(2 * (bits + 1))
        for s in range(2):
            sm_send[s] = small[s]
            for k in range(half // 128):
                low = s * half + k * 128
                sm_send[s, k : k + 1, :] = gg[0:1, low : low + 128]

        def swap(k):
            if k == 0:
                src, key = sm_send.at[1 - me.shard], "x"
            else:
                src, key = sm_sum, k - 1
            return pltpu.make_async_remote_copy(
                src, sm_recv.at[k], sem_ref.at[base + 2 * k], sem_ref.at[base + 2 * k + 1],
                device_id=me.partner(key), device_id_type=pl.DeviceIdType.MESH,
            )

        swap(0).start()
        events = ending
        share = -(-len(events) // (bits + 2))
        for k in range(bits + 1):
            run(events[k * share : (k + 1) * share])
            swap(k).wait()
            if k == 0:
                sm_sum[...] = sm_send[me.shard] + sm_recv[0]
            else:
                sm_sum[...] += sm_recv[k]
            if k < bits:
                swap(k + 1).start()
        run(events[(bits + 1) * share :])
        small_out[...] = sm_sum[...]


def tail(dz, dxd, u, g, gain, w_t, wb_own, wz_oth, wx_oth, wb_oth, go_hand, gz_hand, gx, small):
    bits = rep_bits()
    tokens = dz.shape[0]
    rows = TAIL_ROWS
    by_row = lambda i: (i, 0)
    fixed = lambda i: (0, 0)
    hbm = pl.BlockSpec(memory_space=pl.ANY)
    sds = jax.ShapeDtypeStruct
    half = D // 2
    scratch = []
    for height in (DI, DI, 384, DI, DI, 384):
        scratch.append(pltpu.VMEM((height, half), BF))
    scratch += [
        pltpu.VMEM((8, D), F32),
        pltpu.VMEM((rows, D), F32),
        pltpu.VMEM((2, VEC, 128), F32),
        pltpu.VMEM((VEC, 128), F32),
        pltpu.VMEM((bits + 1, VEC, 128), F32),
    ]
    scratch += plan_scratch(bits, tail_plan())
    scratch.append(pltpu.SemaphoreType.DMA((1400,)))
    return pl.pallas_call(
        functools.partial(tail_kernel, bits),
        grid=(tokens // rows,),
        in_specs=[
            pl.BlockSpec((rows, DI), by_row),
            pl.BlockSpec((rows, XD), by_row),
            pl.BlockSpec((rows, D), by_row),
            pl.BlockSpec((rows, D), by_row),
            pl.BlockSpec((1, D), fixed),
        ]
        + [hbm] * 8
        + [pl.BlockSpec((2, VEC, 128), lambda i: (0, 0, 0))],
        out_specs=[
            pl.BlockSpec((rows, D), by_row),
            pl.BlockSpec((8, D), fixed),
            hbm, hbm, hbm, hbm,
            pl.BlockSpec((VEC, 128), fixed),
        ],
        out_shape=[
            sds((tokens, D), F32),
            sds((8, D), F32),
            part_array("go", 3 - to_end("go")),
            part_array("gz", 4 - to_end("gz")),
            part_array("gx", 4),
            part_array("gb", 1),
            sds((VEC, 128), F32),
        ],
        scratch_shapes=scratch,
        compiler_params=pltpu.CompilerParams(
            dimension_semantics=("arbitrary",), collective_id=2, has_side_effects=True,
            vmem_limit_bytes=62 << 20,
        ),
        cost_estimate=pl.CostEstimate(
            flops=20_500_000_000, bytes_accessed=80_000_000, transcendentals=1024
        ),
        name="tail",
    )(
        dz, dxd, u, g, gain, w_t, wb_own, wz_oth, wx_oth, wb_oth, go_hand, gz_hand,
        gx.reshape(5, 2, 2, 2, 48, D), small,
    )


def contract_rows(left, right):
    left, right = left.reshape(-1, left.shape[2]), right.reshape(-1, right.shape[2])
    return lax.dot_general(
        left, right, (((0,), (0,)), ((), ())), preferred_element_type=F32
    ).astype(BF)


def body(
    hidden_in, segment_ids, norm_gain, in_weight, conv_weight, conv_bias, dt_bias, a_log, d_skip,
    gate_gain, out_weight, cotangent,
):
    shard = lax.axis_index("shard")
    tokens = hidden_in.shape[0]
    chunks = tokens // Q

    small = [norm_gain, conv_bias, dt_bias, a_log, d_skip, gate_gain, conv_weight.reshape(-1)]
    vector = jnp.concatenate(small)
    vector = jnp.pad(vector, (0, VEC * 128 - vector.shape[0])).reshape(VEC, 128)
    w_t = in_weight.T
    w_b = jnp.pad(w_t[2 * DI :], ((0, 384 - (CW - DI) - H), (0, 0)))
    wx, wb, both, normed2, g2, raw, xd = gather(hidden_in, vector, w_t, w_b, cotangent)
    wx, wb = wx.reshape(DI, -1), wb.reshape(384, -1)

    both = both.reshape(2, VEC * 128)
    whole, at = [], 0
    for value in small:
        whole.append(both[:, at : at + value.size])
        at += value.size
    gain, cbias, dtb, alog, skip, ggain = [v.reshape(-1) for v in whole[:6]]
    cweight = whole[6].reshape(2, CONV, CW // 2).transpose(1, 0, 2).reshape(CONV, CW)
    prm = jnp.concatenate(
        [
            jnp.pad(cweight, ((0, 0), (0, XD - CW))),
            jnp.pad(cbias, (0, XD - CW))[None],
            jnp.pad(jnp.repeat(skip, HEADDIM), (0, XD - DI))[None],
            jnp.pad(dtb, (0, XD - H))[None],
            jnp.pad(alog, (0, XD - H))[None],
        ]
    )
    seg = segment_ids.reshape(tokens)
    none = jnp.full((3,), -1, jnp.int32)
    before = jnp.concatenate([none, seg])
    after = jnp.concatenate([seg, none])
    by_chunk = seg.reshape(chunks, Q)
    last = by_chunk[:, -1:]
    earlier = jnp.concatenate([none[:1, None], last[:-1]])
    columns = [seg]
    columns += [before[3 - k : 3 - k + tokens] == seg for k in (1, 2, 3)]
    columns += [(by_chunk == earlier).reshape(-1), (by_chunk == last).reshape(-1)]
    columns += [after[k : k + tokens] == seg for k in (1, 2, 3)]
    columns += [jnp.zeros_like(seg)] * 7
    segc = jnp.stack([v.astype(F32) for v in columns], axis=1)
    segr = jnp.broadcast_to(by_chunk.astype(F32)[:, None, :], (chunks, 8, Q))

    ind, ind2, ind_t, rho_t = spread_consts()
    cum3, ex, cumt = prep(raw, prm, segc)
    y, sin, conv, wz, wo = scan_fwd(
        xd, segc, segr, cum3, ex, cumt, prm, ind, ind2, w_t, out_weight
    )
    wz, wo = wz.reshape(DI, -1), wo.reshape(DI // 2, D)
    gn2, dz2, dz, dy, block_out, gg = gate(
        y, normed2, cotangent, hidden_in, w_t, wz, out_weight, wo, ggain[None, :]
    )
    go = contract_rows(gn2, g2)
    gz = contract_rows(dz2, normed2)
    dxd, dx2, pg, go_hand, gz_hand, go0, gz0 = scan_bwd(
        xd, conv, dy, sin, segc, segr, cum3, ex, cumt, prm, ind, ind2, ind_t, rho_t, go, gz
    )
    gx = contract_rows(dx2, normed2)
    grads = [
        jnp.zeros((D,), F32), pg[4, :CW], pg[6, :H], pg[7, :H], pg[5, :DI].reshape(H, HEADDIM).sum(1), gg[0],
        pg[:CONV, :CW].reshape(CONV, 2, CW // 2).transpose(1, 0, 2).reshape(2, -1),
    ]
    packed = jnp.concatenate([v.reshape(2, -1) for v in grads], axis=1)
    packed = jnp.pad(packed, ((0, 0), (0, VEC * 128 - packed.shape[1]))).reshape(2, VEC, 128)
    input_grad, _, go1, gz1, gx, gb, packed = tail(
        dz, dxd, hidden_in, cotangent, gain[None, :], w_t, w_b, wz, wx, wb, go_hand, gz_hand,
        gx, packed,
    )
    own_inner, own_outer = widen(gz0, gz1, gx, gb, go0, go1)
    packed = packed.reshape(-1)
    owned, at = [], 0
    for value in small:
        owned.append(packed[at : at + value.size])
        at += value.size
    own_gain, own_cbias, own_dtb, own_alog, own_skip, own_gg, own_cw = owned
    return (
        block_out, input_grad, own_gain, own_inner.T, own_cw.reshape(conv_weight.shape), own_cbias,
        own_dtb, own_alog, own_skip, own_gg, own_outer,
    )


def solution(mesh):
    rows, half = P(("rep", "shard"), None), P("shard")
    wide, taps = P("shard", None), P(None, "shard")
    in_specs = (rows, rows, half, wide, taps, half, half, half, half, half, wide, rows)
    out_specs = (rows, rows, half, wide, taps, half, half, half, half, half, wide)
    return jax.shard_map(body, mesh=mesh, in_specs=in_specs, out_specs=out_specs, check_vma=False)
```
